1024 devices in a mesh: px: 4 (over z_lo), py: 16 (over y, z_hi), depth: 16 (over x, core).
Axes of the slice: x: 8, y: 8, z: 8 (z_hi: 2, z_lo: 4; z = z_hi * 4 + z_lo), core: 2. Of those that a mesh axis runs over, the one named last changes fastest.
Arguments:
- tokens: bfloat16 [3072, 7168], P('depth', ('py', 'px')), may hold values from -6 to 6
- up_weight: bfloat16 [7168, 32768], P('py', ('px', 'depth')), may hold values from -0.1875 to 0.1875
- up_bias: bfloat16 [32768], P(('px', 'py')), may hold values from -3 to 3
Outputs:
- hidden: bfloat16 [3072, 32768], P('depth', ('px', 'py'))
The draws below stay inside these ranges and needn't reach their ends.
All inputs are finite; a program needn't handle non-finite values.
Results may differ from the reference program's by a relative error of at most 0.022.
Values may be sent and summed in bfloat16 or wider, within the bound.
A program may use at most 32 MiB of HBM per device.

```python
import jax
import jax.numpy as jnp
from jax import lax

D = 7168
FF = 32768
TOKENS = 3072
N_PY = 16


def with_spikes(drawn, stream_key, source, target, shards_of, factor):
    def block_of(axis_at):
        return (jnp.arange(drawn.shape[axis_at]) // (drawn.shape[axis_at] // shards_of)).reshape((-1,) + (1,) * (drawn.ndim - 1 - axis_at))

    near = jax.random.permutation(stream_key, shards_of)[block_of(target)]
    second = (block_of(target) + shards_of // 2) % shards_of
    return jnp.where((block_of(source) == near) | (block_of(source) == second), factor * drawn, drawn)


def block_scale(own_key, extent, shards, smallest, largest):
    loudness = 1.0
    for dim, parts in shards:
        draws = jax.random.uniform(jax.random.fold_in(jax.random.fold_in(own_key, 6), dim), (parts,), jnp.float32, smallest / len(shards), largest / len(shards))
        loudness = loudness * jnp.repeat(jnp.exp(draws), extent[dim] // parts).reshape((-1,) + (1,) * (len(extent) - 1 - dim))
    return loudness


def bell_draw(own_key, shape, deviation, limit, split=(), held_as=jnp.bfloat16):
    values = jax.random.normal(own_key, shape, jnp.float32) * deviation
    if len(split) > 0:
        values = block_scale(own_key, shape, split, -0.22, 0.18) * values
    return jnp.clip(values, min=-limit, max=limit).astype(held_as)


def noise_with(key, shape, deviation, most, split, heavy, kind=jnp.bfloat16):
    values = deviation * jax.random.normal(key, shape, jnp.float32)
    if split:
        values = values * block_scale(key, shape, split, -0.22, 0.18)
    return jnp.clip(with_spikes(values, jax.random.fold_in(key, 3), *heavy), -most, most).astype(kind)


def setup_inputs(seed: int = 0) -> dict:
    key_of = jax.random.split(jax.random.key(seed), 4)
    return {
        "tokens": bell_draw(key_of[0], (TOKENS, D), 1.0, 6.0, ((0, 16), (1, 64))),
        "up_weight": noise_with(key_of[1], (D, FF), D ** -0.5, 0.1875, ((0, 16), (1, 64)), (0, 1, 64, 4.0)),
        "up_bias": bell_draw(key_of[2], (FF,), 0.5, 3.0, ((0, 64),)),
    }


def reference(tokens, up_weight, up_bias):
    feature_blocks = tokens.reshape(TOKENS, N_PY, D // N_PY).transpose(1, 0, 2)
    weight_blocks = up_weight.reshape(N_PY, D // N_PY, FF)

    def accumulate(total, blocks):
        feature_block, weight_block = blocks
        partial_value = jnp.dot(feature_block, weight_block, preferred_element_type=jnp.float32).astype(jnp.bfloat16)
        partial_value = lax.optimization_barrier(partial_value)
        return total + partial_value.astype(jnp.float32), None

    start_total = jnp.zeros((TOKENS, FF), jnp.float32)
    total, unused = lax.scan(accumulate, start_total, (feature_blocks, weight_blocks))
    summed = total + up_bias.astype(jnp.float32)[None, :]
    return jax.nn.gelu(summed, approximate=True).astype(jnp.bfloat16)
```

```python
import jax
import jax.numpy as jnp
from jax import lax
from jax.experimental import pallas as pl
from jax.experimental.pallas import tpu as pltpu
from jax.sharding import PartitionSpec as P

MESH = pl.DeviceIdType.MESH
BF16, F32 = jnp.bfloat16, jnp.float32
N = 8
ROWS = 192
PIECES = 16
COLS = 256
HALF = 224
FEAT = 112
AHEAD = 8
LAG = 2


def device(x, core, y, z_hi, z_lo):
    return (z_lo, y * 2 + z_hi, x * 2 + core)


def piece_of(i):
    j = jnp.maximum(i - 2, 0)
    own = jnp.where(i < 2, 1, 0)
    hops = (1 - own) * (j // 4 + 1)
    r = j % 4
    far = hops // 4
    way = (1 - own) * (r % 2)
    half = own * i + (1 - own) * (far * r + (1 - far) * (r // 2))
    return hops, way, half


def kernel(
    t_ref, w_ref, b_ref, o_ref,
    t_in, t_cat, w_all, own_part, sib_out, sib_in, y_out, y_in, total,
    t_send, t_recv, swap_send, local_sem, w_send, w_recv, sib_send, sib_recv, y_send, y_recv,
):
    px, py, depth = lax.axis_index("px"), lax.axis_index("py"), lax.axis_index("depth")
    x, c = depth // 2, depth % 2
    y, zh, zl = py // 2, py % 2, px
    z = zh * 4 + zl
    near = jnp.where(c == zh, 1, 0)

    barrier = pltpu.get_barrier_semaphore()

    def greet(target):
        pl.semaphore_signal(barrier, inc=1, device_id=target, device_id_type=MESH)

    greet(device((x + 1) % N, c, y, zh, zl))
    greet(device((x + N - 1) % N, c, y, zh, zl))
    greet(device(x, 1 - c, y, zh, zl))
    greet(device(x, zh, y, 1 - zh, zl))
    for ct in range(2):
        for kz in range(2):
            for b in range(2):
                zl_from = 2 * c + b

                @pl.when((kz != zh) | (zl_from != zl))
                def _(ct=ct, kz=kz, zl_from=zl_from):
                    greet(device(x, ct, y, kz, zl_from))

    for dy in range(1, N):
        greet(device(x, c, (y + dy) % N, zh, zl))
    pl.semaphore_wait(barrier, 3 + 2 * (1 - near) + 7 + 7)

    def swap(h, q, remote):
        src = w_ref.at[pl.ds(h * HALF, HALF), pl.ds(q * COLS, COLS)]
        part = 1 - near
        dst = w_all.at[0, q, pl.ds(pl.multiple_of(part * HALF, HALF), HALF)]
        if remote:
            return pltpu.make_async_remote_copy(
                src_ref=src, dst_ref=dst, send_sem=swap_send.at[h, q], recv_sem=w_recv.at[0, part, q],
                device_id=device(x, h, y, c, zl), device_id_type=MESH)
        return pltpu.make_async_copy(src, dst, local_sem.at[q])

    def swap_all(run_remote, run_local):
        for q in range(2):
            for h in range(2):
                here = (c == zh) & (c == h)
                if run_local is not None:
                    @pl.when(here)
                    def _(h=h, q=q):
                        run_local(swap(h, q, False))

                @pl.when(jnp.logical_not(here))
                def _(h=h, q=q):
                    run_remote(swap(h, q, True))

    t_core = zl // 2
    b_mine = zl % 2

    def t_copy(dz):
        zd = (z + dz) % N
        zhd = zd // 4
        other = jnp.where(c == t_core, 0, 1)
        rel = jnp.where(zhd == zh, 0, 1)
        return pltpu.make_async_remote_copy(
            src_ref=t_ref, dst_ref=t_in.at[other, rel * 2 + b_mine], send_sem=t_send.at[dz],
            recv_sem=t_recv.at[other, rel * 2 + b_mine],
            device_id=device(x, t_core, y, zhd, zd % 4), device_id_type=MESH)

    def t_local():
        return pltpu.make_async_copy(t_ref, t_in.at[0, b_mine], local_sem.at[2])

    def send_tokens():
        for dz in (4, 3, 5, 2, 6, 1, 7):
            t_copy(dz).start()

        @pl.when(c != t_core)
        def _():
            t_copy(0).start()

        @pl.when(c == t_core)
        def _():
            t_local().start()

    @pl.when(c == zh)
    def _():
        swap_all(lambda d: d.start(), lambda d: d.start())
        send_tokens()

    @pl.when(c != zh)
    def _():
        send_tokens()
        swap_all(lambda d: d.start(), None)

    def w_copy(hops, way, part, half):
        rows = pl.ds(pl.multiple_of(part * HALF, HALF), HALF)
        slot = hops + 4 * way * jnp.where(hops > 0, 1, 0)
        to = hops + 1 + 4 * way
        return pltpu.make_async_remote_copy(
            src_ref=w_all.at[slot, half, rows], dst_ref=w_all.at[to, half, rows],
            send_sem=w_send.at[to, part, half], recv_sem=w_recv.at[to, part, half],
            device_id=device((x + 1 + 6 * way) % N, c, y, zh, zl), device_id_type=MESH)

    def w_arrived(slot, part, half):
        rows = pl.ds(pl.multiple_of(part * HALF, HALF), HALF)
        ref = w_all.at[slot, half, rows]
        pltpu.make_async_copy(ref, ref, w_recv.at[slot, part, half]).wait()

    def forward(i, part):
        hops, way, half = piece_of(i)
        slot = hops + 4 * way

        if part == 0:
            @pl.when((i < 2) & (c == zh))
            def _():
                ref = w_all.at[0, half, pl.ds(0, HALF)]
                pltpu.make_async_copy(ref, ref, local_sem.at[half]).wait()

            @pl.when((i >= 2) | (c != zh))
            def _():
                w_arrived(slot, 0, half)
        else:
            w_arrived(slot, 1, half)

        @pl.when((hops < 3) | ((hops == 3) & (half == way)))
        def _():
            w_copy(hops, way, part, half).start()

        @pl.when(hops == 0)
        def _():
            w_copy(hops, way + 1, part, half).start()

    def sib_copy(i):
        return pltpu.make_async_remote_copy(
            src_ref=sib_out.at[i], dst_ref=sib_in.at[i], send_sem=sib_send.at[i], recv_sem=sib_recv.at[i],
            device_id=device(x, 1 - c, y, zh, zl), device_id_type=MESH)

    def product(i):
        hops, way, half = piece_of(i)
        w = w_all[hops + 4 * way, half]
        sib_out[i] = jnp.dot(t_cat[1], w, preferred_element_type=F32).astype(BF16)
        sib_copy(i).start()
        own_part[i] = jnp.dot(t_cat[0], w, preferred_element_type=F32)

    def y_step(i):
        hops, way, half = piece_of(i)
        owner = (x + N + hops * (2 * way - 1)) % N
        return (owner + N - y) % N, half

    def y_copy(i, dy, half):
        return pltpu.make_async_remote_copy(
            src_ref=y_out.at[i], dst_ref=y_in.at[dy, half], send_sem=y_send.at[i], recv_sem=y_recv.at[dy, half],
            device_id=device(x, c, (y + dy) % N, zh, zl), device_id_type=MESH)

    def onward(i):
        sib_copy(i).wait_recv()
        dy, half = y_step(i)
        value = own_part[i] + sib_in[i].astype(F32)

        @pl.when(dy == 0)
        def _():
            total[half] = value

        @pl.when(dy != 0)
        def _():
            y_out[i] = value.astype(BF16)
            y_copy(i, dy, half).start()

    def lead(i, carry):
        forward(i, 0)
        return carry

    lax.fori_loop(0, AHEAD, lead, 0)

    for other in range(2):
        for s in range(4):
            mine = (other == 0) & (s == b_mine) & (c == t_core)

            @pl.when(mine)
            def _():
                t_local().wait()

            @pl.when(jnp.logical_not(mine))
            def _(other=other, s=s):
                ref = t_in.at[other, s]
                pltpu.make_async_copy(ref, ref, t_recv.at[other, s]).wait()

        t_cat[other] = jnp.concatenate([t_in[other, s] for s in range(4)], axis=-1)

    def step(i, carry):
        @pl.when(i < PIECES)
        def _():
            forward(i, 1)

        @pl.when(i + AHEAD < PIECES)
        def _():
            forward(i + AHEAD, 0)

        @pl.when(i < PIECES)
        def _():
            product(i)

        @pl.when(i >= LAG)
        def _():
            onward(i - LAG)

        return carry

    lax.fori_loop(0, PIECES + LAG, step, 0)

    def take(k, carry):
        dy, half = k // 2 + 1, k % 2
        ref = y_in.at[dy, half]
        pltpu.make_async_copy(ref, ref, y_recv.at[dy, half]).wait()
        return carry

    lax.fori_loop(0, 14, take, 0)
    for half in range(2):
        value = total[half]
        for dy in range(1, N):
            value = value + y_in[dy, half].astype(F32)
        value = value + b_ref[0:1, half * COLS:(half + 1) * COLS].astype(F32)
        inner = 0.7978845608028654 * (value + 0.044715 * (value * value * value))
        o_ref[:, half * COLS:(half + 1) * COLS] = (0.5 * value * (1.0 + jnp.tanh(inner))).astype(BF16)

    for dz in range(1, N):
        t_copy(dz).wait_send()

    @pl.when(c != t_core)
    def _():
        t_copy(0).wait_send()

    swap_all(lambda d: d.wait_send(), None)

    def done(i, carry):
        hops, way, half = piece_of(i)
        for part in range(2):
            @pl.when((hops < 3) | ((hops == 3) & (half == way)))
            def _():
                w_copy(hops, way, part, half).wait_send()

            @pl.when(hops == 0)
            def _():
                w_copy(hops, way + 1, part, half).wait_send()

        sib_copy(i).wait_send()
        dy, half = y_step(i)

        @pl.when(dy != 0)
        def _():
            y_copy(i, dy, half).wait_send()

        return carry

    lax.fori_loop(0, PIECES, done, 0)


def body(tokens, up_weight, up_bias):
    return pl.pallas_call(
        kernel,
        out_shape=jax.ShapeDtypeStruct((ROWS, 512), BF16),
        in_specs=[
            pl.BlockSpec(memory_space=pltpu.VMEM),
            pl.BlockSpec(memory_space=pltpu.VMEM),
            pl.BlockSpec(memory_space=pltpu.VMEM),
        ],
        out_specs=pl.BlockSpec(memory_space=pltpu.VMEM),
        scratch_shapes=[
            pltpu.VMEM((2, 4, ROWS, FEAT), BF16),
            pltpu.VMEM((2, ROWS, 4 * FEAT), BF16),
            pltpu.VMEM((9, 2, 2 * HALF, COLS), BF16),
            pltpu.VMEM((PIECES, ROWS, COLS), F32),
            pltpu.VMEM((PIECES, ROWS, COLS), BF16),
            pltpu.VMEM((PIECES, ROWS, COLS), BF16),
            pltpu.VMEM((PIECES, ROWS, COLS), BF16),
            pltpu.VMEM((N, 2, ROWS, COLS), BF16),
            pltpu.VMEM((2, ROWS, COLS), F32),
            pltpu.SemaphoreType.DMA((N,)),
            pltpu.SemaphoreType.DMA((2, 4)),
            pltpu.SemaphoreType.DMA((2, 2)),
            pltpu.SemaphoreType.DMA((3,)),
            pltpu.SemaphoreType.DMA((9, 2, 2)),
            pltpu.SemaphoreType.DMA((9, 2, 2)),
            pltpu.SemaphoreType.DMA((PIECES,)),
            pltpu.SemaphoreType.DMA((PIECES,)),
            pltpu.SemaphoreType.DMA((PIECES,)),
            pltpu.SemaphoreType.DMA((N, 2)),
        ],
        name="up_proj",
        compiler_params=pltpu.CompilerParams(
            collective_id=0, has_side_effects=True, vmem_limit_bytes=40 * 2**20
        ),
    )(tokens, up_weight, up_bias.reshape(1, 512))


def solution(mesh):
    return jax.shard_map(
        body,
        mesh=mesh,
        in_specs=(P("depth", ("py", "px")), P("py", ("px", "depth")), P(("px", "py"))),
        out_specs=P("depth", ("px", "py")),
        check_vma=False,
    )
```

```python
import jax
import jax.numpy as jnp
from jax import lax
from jax.experimental import pallas as pl
from jax.experimental.pallas import tpu as pltpu
from jax.sharding import PartitionSpec as P

MESH = pl.DeviceIdType.MESH
BF16, F32 = jnp.bfloat16, jnp.float32
N = 8
ROWS = 192
PIECES = 16
COLS = 256
HALF = 224
FEAT = 112
NEAR_AT, FAR_AT, PRODUCT_AT, PAIR_AT, JOIN_AT, OWNER_AT = 0, 8, 11, 13, 20, 28
TOKENS_AT = 9


def device(x, core, y, z_hi, z_lo):
    return (z_lo, y * 2 + z_hi, x * 2 + core)


def piece_of(i):
    if i < 2:
        return 0, 0, i
    hops, r = (i - 2) // 4 + 1, (i - 2) % 4
    return hops, r % 2, r if hops == 4 else r // 2


def kernel(
    t_ref, w_ref, b_ref, o_ref,
    t_in, t_cat, w_all, own_part, sib_out, sib_in, y_out, y_in,
    t_send, t_recv, swap_send, local_sem, w_send, w_recv, sib_send, sib_recv, y_send, y_recv,
):
    px, py, depth = lax.axis_index("px"), lax.axis_index("py"), lax.axis_index("depth")
    x, c = depth // 2, depth % 2
    y, zh, zl = py // 2, py % 2, px
    z = zh * 4 + zl
    x_right, x_left = (x + 1) % N, (x + N - 1) % N
    near = jnp.where(c == zh, 1, 0)

    barrier = pltpu.get_barrier_semaphore()

    def greet(target):
        pl.semaphore_signal(barrier, inc=1, device_id=target, device_id_type=MESH)

    greet(device((x + 1) % N, c, y, zh, zl))
    greet(device((x + N - 1) % N, c, y, zh, zl))
    greet(device(x, 1 - c, y, zh, zl))
    greet(device(x, zh, y, 1 - zh, zl))
    for ct in range(2):
        for kz in range(2):
            for b in range(2):
                zl_from = 2 * c + b

                @pl.when((kz != zh) | (zl_from != zl))
                def _(ct=ct, kz=kz, zl_from=zl_from):
                    greet(device(x, ct, y, kz, zl_from))

    for dy in (1, 2, 6, 7):
        greet(device(x, c, (y + dy) % N, zh, zl))
    pl.semaphore_wait(barrier, 3 + 2 * (1 - near) + 7 + 4)

    def swap(h, q, remote):
        src = w_ref.at[pl.ds(h * HALF, HALF), pl.ds(q * COLS, COLS)]
        part = 1 - near
        dst = w_all.at[0, q, pl.ds(pl.multiple_of(part * HALF, HALF), HALF)]
        if remote:
            return pltpu.make_async_remote_copy(
                src_ref=src, dst_ref=dst, send_sem=swap_send.at[h, q], recv_sem=w_recv.at[0, part, q],
                device_id=device(x, h, y, c, zl), device_id_type=MESH)
        return pltpu.make_async_copy(src, dst, local_sem.at[q])

    def swap_all(run_remote, run_local):
        for q in range(2):
            for h in range(2):
                here = (c == zh) & (c == h)
                if run_local is not None:
                    @pl.when(here)
                    def _(h=h, q=q):
                        run_local(swap(h, q, False))

                @pl.when(jnp.logical_not(here))
                def _(h=h, q=q):
                    run_remote(swap(h, q, True))

    t_core = zl // 2
    b_mine = zl % 2

    def t_copy(dz):
        zd = (z + dz) % N
        zhd = zd // 4
        other = jnp.where(c == t_core, 0, 1)
        rel = jnp.where(zhd == zh, 0, 1)
        return pltpu.make_async_remote_copy(
            src_ref=t_ref, dst_ref=t_in.at[other, rel * 2 + b_mine], send_sem=t_send.at[dz],
            recv_sem=t_recv.at[other, rel * 2 + b_mine],
            device_id=device(x, t_core, y, zhd, zd % 4), device_id_type=MESH)

    def t_local():
        return pltpu.make_async_copy(t_ref, t_in.at[0, b_mine], local_sem.at[2])

    def send_tokens():
        for dz in (4, 3, 5, 2, 6, 1, 7):
            t_copy(dz).start()

        @pl.when(c != t_core)
        def _():
            t_copy(0).start()

        @pl.when(c == t_core)
        def _():
            t_local().start()

    swap_all(lambda d: d.start(), lambda d: d.start())

    def w_copy(hops, way, part, half):
        rows = pl.ds(part * HALF, HALF)
        slot = hops + 4 * way if hops else 0
        to = hops + 1 + 4 * way
        return pltpu.make_async_remote_copy(
            src_ref=w_all.at[slot, half, rows], dst_ref=w_all.at[to, half, rows],
            send_sem=w_send.at[to, part, half], recv_sem=w_recv.at[to, part, half],
            device_id=device(x_left if way else x_right, c, y, zh, zl), device_id_type=MESH)

    def w_arrived(slot, part, half):
        ref = w_all.at[slot, half, pl.ds(part * HALF, HALF)]
        pltpu.make_async_copy(ref, ref, w_recv.at[slot, part, half]).wait()

    def onward_ways(hops, way, half):
        if hops == 0:
            return (0, 1)
        return (way,) if hops < 3 or (hops == 3 and half == way) else ()

    def forward(i, part):
        hops, way, half = piece_of(i)
        slot = hops + 4 * way

        if part == 0 and i < 2:
            @pl.when(c == zh)
            def _():
                ref = w_all.at[0, half, pl.ds(0, HALF)]
                pltpu.make_async_copy(ref, ref, local_sem.at[half]).wait()

            @pl.when(c != zh)
            def _():
                w_arrived(slot, 0, half)
        else:
            w_arrived(slot, part, half)
        for leave in onward_ways(hops, way, half):
            w_copy(hops, leave, part, half).start()

    def sib_copy(i):
        return pltpu.make_async_remote_copy(
            src_ref=sib_out.at[i], dst_ref=sib_in.at[i], send_sem=sib_send.at[i], recv_sem=sib_recv.at[i],
            device_id=device(x, 1 - c, y, zh, zl), device_id_type=MESH)

    def product(i):
        hops, way, half = piece_of(i)
        w = w_all[hops + 4 * way, half]
        sib_out[i] = jnp.dot(t_cat[1], w, preferred_element_type=F32).astype(BF16)
        sib_copy(i).start()
        own_part[i] = jnp.dot(t_cat[0], w, preferred_element_type=F32)

    def y_role(i):
        hops, way, half = piece_of(i)
        owner = (x + N + hops * (2 * way - 1)) % N
        return (N + (y - owner) * (1 - 2 * half)) % N, half

    def pass_on(i, role, half):
        to_second = jnp.where((role == 3) | (role == 7), 1, 0)
        step = jnp.where(role == 3, -2, jnp.where(role >= 5, 1, -1)) * (1 - 2 * half)
        return pltpu.make_async_remote_copy(
            src_ref=y_out.at[i], dst_ref=y_in.at[i, to_second], send_sem=y_send.at[i], recv_sem=y_recv.at[i, to_second],
            device_id=device(x, c, (y + N + step) % N, zh, zl), device_id_type=MESH)

    def received(i, k):
        ref = y_in.at[i, k]
        pltpu.make_async_copy(ref, ref, y_recv.at[i, k]).wait()
        return y_in[i, k].astype(F32)

    def pair_step(i):
        sib_copy(i).wait_recv()
        role, half = y_role(i)
        value = own_part[i] + sib_in[i].astype(F32)
        leaf = (role == 4) | (role == 2) | (role == 5)

        @pl.when(leaf)
        def _():
            y_out[i] = value.astype(BF16)
            pass_on(i, role, half).start()

        @pl.when(jnp.logical_not(leaf))
        def _():
            own_part[i] = value

    def join_step(i):
        role, half = y_role(i)

        @pl.when((role == 3) | (role == 6))
        def _():
            y_out[i] = (own_part[i] + received(i, 0)).astype(BF16)
            pass_on(i, role, half).start()

    def owner_step(i):
        role, half = y_role(i)

        @pl.when((role == 1) | (role == 7))
        def _():
            value = own_part[i] + received(i, 0)

            @pl.when(role == 1)
            def _():
                y_out[i] = (value + received(i, 1)).astype(BF16)

            @pl.when(role == 7)
            def _():
                y_out[i] = value.astype(BF16)

            pass_on(i, role, half).start()

    def result(i):
        role, half = y_role(i)

        @pl.when(role == 0)
        def _():
            value = own_part[i] + received(i, 0) + received(i, 1)
            value = value + b_ref[half * COLS:(half + 1) * COLS].astype(F32)[None, :]
            inner = 0.7978845608028654 * (value + 0.044715 * (value * value * value))
            o_ref[:, half * COLS:(half + 1) * COLS] = (0.5 * value * (1.0 + jnp.tanh(inner))).astype(BF16)

    def take_tokens():
        for other in range(2):
            for s in range(4):
                mine = (other == 0) & (s == b_mine) & (c == t_core)

                @pl.when(mine)
                def _():
                    t_local().wait()

                @pl.when(jnp.logical_not(mine))
                def _(other=other, s=s):
                    ref = t_in.at[other, s]
                    pltpu.make_async_copy(ref, ref, t_recv.at[other, s]).wait()

            t_cat[other] = jnp.concatenate([t_in[other, s] for s in range(4)], axis=-1)

    for t in range(PIECES + OWNER_AT):
        for offset, act in (
            (NEAR_AT, lambda i: forward(i, 0)),
            (FAR_AT, lambda i: forward(i, 1)),
            (PRODUCT_AT, product),
            (PAIR_AT, pair_step),
            (JOIN_AT, join_step),
            (OWNER_AT, owner_step),
        ):
            if act is product and t == PRODUCT_AT:
                take_tokens()
            if offset <= t < offset + PIECES:
                act(t - offset)
        if t == TOKENS_AT:
            send_tokens()

    for dz in range(1, N):
        t_copy(dz).wait_send()

    @pl.when(c != t_core)
    def _():
        t_copy(0).wait_send()

    swap_all(lambda d: d.wait_send(), None)

    for i in range(PIECES):
        hops, way, half = piece_of(i)
        for part in range(2):
            for leave in onward_ways(hops, way, half):
                w_copy(hops, leave, part, half).wait_send()
        sib_copy(i).wait_send()
        role, half = y_role(i)

        @pl.when(role != 0)
        def _():
            pass_on(i, role, half).wait_send()

    for i in range(PIECES):
        result(i)


def body(tokens, up_weight, up_bias):
    return pl.pallas_call(
        kernel,
        out_shape=jax.ShapeDtypeStruct((ROWS, 512), BF16),
        in_specs=[
            pl.BlockSpec(memory_space=pltpu.HBM),
            pl.BlockSpec(memory_space=pltpu.HBM),
            pl.BlockSpec(memory_space=pltpu.VMEM),
        ],
        out_specs=pl.BlockSpec(memory_space=pltpu.VMEM),
        scratch_shapes=[
            pltpu.VMEM((2, 4, ROWS, FEAT), BF16),
            pltpu.VMEM((2, ROWS, 4 * FEAT), BF16),
            pltpu.VMEM((9, 2, 2 * HALF, COLS), BF16),
            pltpu.VMEM((PIECES, ROWS, COLS), F32),
            pltpu.VMEM((PIECES, ROWS, COLS), BF16),
            pltpu.VMEM((PIECES, ROWS, COLS), BF16),
            pltpu.VMEM((PIECES, ROWS, COLS), BF16),
            pltpu.VMEM((PIECES, 2, ROWS, COLS), BF16),
            pltpu.SemaphoreType.DMA((N,)),
            pltpu.SemaphoreType.DMA((2, 4)),
            pltpu.SemaphoreType.DMA((2, 2)),
            pltpu.SemaphoreType.DMA((3,)),
            pltpu.SemaphoreType.DMA((9, 2, 2)),
            pltpu.SemaphoreType.DMA((9, 2, 2)),
            pltpu.SemaphoreType.DMA((PIECES,)),
            pltpu.SemaphoreType.DMA((PIECES,)),
            pltpu.SemaphoreType.DMA((PIECES,)),
            pltpu.SemaphoreType.DMA((PIECES, 2)),
        ],
        name="up_proj",
        compiler_params=pltpu.CompilerParams(
            collective_id=0, has_side_effects=True, vmem_limit_bytes=40 * 2**20
        ),
    )(tokens, up_weight, up_bias)


def solution(mesh):
    return jax.shard_map(
        body,
        mesh=mesh,
        in_specs=(P("depth", ("py", "px")), P("py", ("px", "depth")), P(("px", "py"))),
        out_specs=P("depth", ("px", "py")),
        check_vma=False,
    )
```

```python
import jax
import jax.numpy as jnp
from jax import lax
from jax.experimental import pallas as pl
from jax.experimental.pallas import tpu as pltpu
from jax.sharding import PartitionSpec as P

MESH = pl.DeviceIdType.MESH
BF16, F32 = jnp.bfloat16, jnp.float32
N = 8
ROWS = 192
PIECES = 16
COLS = 256
HALF = 224
FEAT = 112
PART = 96
STEPS = (
    0, 1, 2, 5, 4, 3, 16, 96, 6, 17, 9, 18, 8, 7, 10, 19, 97, 34, 20, 35,
    21, 11, 33, 32, 12, 37, 36, 23, 51, 22, 49, 38, 53, 50, 48, 13, 52, 39, 54, 24,
    55, 40, 25, 26, 42, 56, 41, 67, 27, 43, 66, 71, 15, 14, 70, 57, 58, 64, 65, 28,
    59, 44, 29, 30, 45, 46, 60, 68, 61, 62, 86, 75, 72, 87, 31, 47, 74, 73, 63, 76,
    84, 69, 77, 78, 88, 83, 80, 89, 85, 79, 82, 81,
)
DEEP = {
    4: (1, -1, 0, 0), 2: (1, -1, 0, 0), 5: (1, 1, 0, 0),
    3: (2, -2, 1, 1), 6: (2, 1, 0, 1), 1: (3, -1, 0, 2), 7: (3, 1, 1, 1),
}
FLAT = {
    4: (1, -1, 0, 0), 2: (1, -1, 0, 0), 5: (1, 1, 0, 0), 7: (1, 1, 2, 0),
    3: (2, -3, 0, 1), 6: (2, 2, 3, 1), 1: (2, -1, 1, 1),
}
DEEP_PIECES = 10


def device(x, core, y, z_hi, z_lo):
    return (z_lo, y * 2 + z_hi, x * 2 + core)


def piece_of(i):
    if i < 2:
        return 0, 0, i
    hops, r = (i - 2) // 4 + 1, (i - 2) % 4
    return hops, r % 2, r if hops == 4 else r // 2


def kernel(
    t_ref, w_ref, b_ref, o_ref,
    t_in, t_cat, w_all, own_part, sib_out, sib_in, y_out, y_in,
    t_send, t_recv, swap_send, local_sem, w_send, w_recv, sib_send, sib_recv, y_send, y_recv,
):
    px, py, depth = lax.axis_index("px"), lax.axis_index("py"), lax.axis_index("depth")
    x, c = depth // 2, depth % 2
    y, zh, zl = py // 2, py % 2, px
    z = zh * 4 + zl
    x_right, x_left = (x + 1) % N, (x + N - 1) % N
    near = jnp.where(c == zh, 1, 0)

    barrier = pltpu.get_barrier_semaphore()

    def greet(target):
        pl.semaphore_signal(barrier, inc=1, device_id=target, device_id_type=MESH)

    greet(device((x + 1) % N, c, y, zh, zl))
    greet(device((x + N - 1) % N, c, y, zh, zl))
    greet(device(x, 1 - c, y, zh, zl))
    greet(device(x, zh, y, 1 - zh, zl))
    for ct in range(2):
        for kz in range(2):
            for b in range(2):
                zl_from = 2 * c + b

                @pl.when((kz != zh) | (zl_from != zl))
                def _(ct=ct, kz=kz, zl_from=zl_from):
                    greet(device(x, ct, y, kz, zl_from))

    for dy in (1, 2, 3, 5, 6, 7):
        greet(device(x, c, (y + dy) % N, zh, zl))
    pl.semaphore_wait(barrier, 3 + 2 * (1 - near) + 7 + 6)

    def swap(h, q, remote):
        src = w_ref.at[pl.ds(h * HALF, HALF), pl.ds(q * COLS, COLS)]
        part = 1 - near
        dst = w_all.at[0, q, pl.ds(pl.multiple_of(part * HALF, HALF), HALF)]
        if remote:
            return pltpu.make_async_remote_copy(
                src_ref=src, dst_ref=dst, send_sem=swap_send.at[h, q], recv_sem=w_recv.at[0, part, q],
                device_id=device(x, h, y, c, zl), device_id_type=MESH)
        return pltpu.make_async_copy(src, dst, local_sem.at[q])

    def swap_all(run_remote, run_local):
        for q in range(2):
            for h in range(2):
                here = (c == zh) & (c == h)
                if run_local is not None:
                    @pl.when(here)
                    def _(h=h, q=q):
                        run_local(swap(h, q, False))

                @pl.when(jnp.logical_not(here))
                def _(h=h, q=q):
                    run_remote(swap(h, q, True))

    t_core = zl // 2
    b_mine = zl % 2

    def t_copy(dz):
        zd = (z + dz) % N
        zhd = zd // 4
        other = jnp.where(c == t_core, 0, 1)
        rel = jnp.where(zhd == zh, 0, 1)
        return pltpu.make_async_remote_copy(
            src_ref=t_ref, dst_ref=t_in.at[other, rel * 2 + b_mine], send_sem=t_send.at[dz],
            recv_sem=t_recv.at[other, rel * 2 + b_mine],
            device_id=device(x, t_core, y, zhd, zd % 4), device_id_type=MESH)

    def t_local():
        return pltpu.make_async_copy(t_ref, t_in.at[0, b_mine], local_sem.at[2])

    def send_tokens():
        for dz in (4, 3, 5, 2, 6, 1, 7):
            t_copy(dz).start()

        @pl.when(c != t_core)
        def _():
            t_copy(0).start()

        @pl.when(c == t_core)
        def _():
            t_local().start()

    swap_all(lambda d: d.start(), lambda d: d.start())

    def w_copy(hops, way, part, half):
        rows = pl.ds(part * HALF, HALF)
        slot = hops + 4 * way if hops else 0
        to = hops + 1 + 4 * way
        return pltpu.make_async_remote_copy(
            src_ref=w_all.at[slot, half, rows], dst_ref=w_all.at[to, half, rows],
            send_sem=w_send.at[to, part, half], recv_sem=w_recv.at[to, part, half],
            device_id=device(x_left if way else x_right, c, y, zh, zl), device_id_type=MESH)

    def w_arrived(slot, part, half):
        ref = w_all.at[slot, half, pl.ds(part * HALF, HALF)]
        pltpu.make_async_copy(ref, ref, w_recv.at[slot, part, half]).wait()

    def onward_ways(hops, way, half):
        if hops == 0:
            return (0, 1)
        return (way,) if hops < 3 or (hops == 3 and half == way) else ()

    def forward(i, part):
        hops, way, half = piece_of(i)
        slot = hops + 4 * way

        if part == 0 and i < 2:
            @pl.when(c == zh)
            def _():
                ref = w_all.at[0, half, pl.ds(0, HALF)]
                pltpu.make_async_copy(ref, ref, local_sem.at[half]).wait()

            @pl.when(c != zh)
            def _():
                w_arrived(slot, 0, half)
        else:
            w_arrived(slot, part, half)
        for leave in onward_ways(hops, way, half):
            w_copy(hops, leave, part, half).start()

    def sib_copy(i):
        return pltpu.make_async_remote_copy(
            src_ref=sib_out.at[i], dst_ref=sib_in.at[i], send_sem=sib_send.at[i], recv_sem=sib_recv.at[i],
            device_id=device(x, 1 - c, y, zh, zl), device_id_type=MESH)

    def product(i):
        hops, way, half = piece_of(i)
        w = w_all[hops + 4 * way, half]
        sib_out[i] = jnp.dot(t_cat[1], w, preferred_element_type=F32).astype(BF16)
        sib_copy(i).start()
        own_part[i] = jnp.dot(t_cat[0], w, preferred_element_type=F32)

    def tree_of(i):
        return DEEP if i < DEEP_PIECES else FLAT

    def climb(i, u, role):
        step, slot = 0, 0
        for r, (_, r_step, r_slot, _) in tree_of(i).items():
            step = jnp.where(role == r, r_step, step)
            slot = jnp.where(role == r, r_slot, slot)
        return pltpu.make_async_remote_copy(
            src_ref=y_out.at[i, u], dst_ref=y_in.at[i, slot, u],
            send_sem=y_send.at[i, u], recv_sem=y_recv.at[i, slot, u],
            device_id=device(x, c, (y + N + step * (1 - 2 * u)) % N, zh, zl), device_id_type=MESH)

    def role_of(i, u):
        hops, way, half = piece_of(i)
        owner = (x + N + hops * (2 * way - 1)) % N
        return (N + (y - owner) * (1 - 2 * u)) % N

    def received(i, k, u):
        ref = y_in.at[i, k, u]
        pltpu.make_async_copy(ref, ref, y_recv.at[i, k, u]).wait()
        return y_in[i, k, u].astype(F32)

    def any_of(role, roles):
        hit = role == roles[0]
        for r in roles[1:]:
            hit = hit | (role == r)
        return hit

    def pair_step(i):
        sib_copy(i).wait_recv()
        leaves = [r for r, v in tree_of(i).items() if v[0] == 1]
        for u in range(2):
            role = role_of(i, u)
            rows = slice(u * PART, (u + 1) * PART)
            value = own_part[i, rows] + sib_in[i, rows].astype(F32)
            leaf = any_of(role, leaves)

            @pl.when(leaf)
            def _():
                y_out[i, u] = value.astype(BF16)
                climb(i, u, role).start()

            @pl.when(jnp.logical_not(leaf))
            def _():
                own_part[i, rows] = value

    def tree_step(i, level):
        for u in range(2):
            role = role_of(i, u)
            rows = slice(u * PART, (u + 1) * PART)
            for count in (1, 2):
                roles = [r for r, v in tree_of(i).items() if v[0] == level and v[3] == count]
                if not roles:
                    continue

                @pl.when(any_of(role, roles))
                def _(count=count):
                    value = own_part[i, rows]
                    for k in range(count):
                        value = value + received(i, k, u)
                    y_out[i, u] = value.astype(BF16)
                    climb(i, u, role).start()

    def result(i):
        _, _, half = piece_of(i)
        cols = slice(half * COLS, (half + 1) * COLS)

        @pl.when(role_of(i, 0) == 0)
        def _():
            for u in range(2):
                rows = slice(u * PART, (u + 1) * PART)
                value = own_part[i, rows]
                for k in range(2 if i < DEEP_PIECES else 4):
                    value = value + received(i, k, u)
                value = value + b_ref[cols].astype(F32)[None, :]
                inner = 0.7978845608028654 * (value + 0.044715 * (value * value * value))
                o_ref[rows, cols] = (0.5 * value * (1.0 + jnp.tanh(inner))).astype(BF16)

    def take_tokens():
        for other in range(2):
            for s in range(4):
                mine = (other == 0) & (s == b_mine) & (c == t_core)

                @pl.when(mine)
                def _():
                    t_local().wait()

                @pl.when(jnp.logical_not(mine))
                def _(other=other, s=s):
                    ref = t_in.at[other, s]
                    pltpu.make_async_copy(ref, ref, t_recv.at[other, s]).wait()

            t_cat[other] = jnp.concatenate([t_in[other, s] for s in range(4)], axis=-1)

    for code in STEPS:
        kind, i = code // 16, code % 16
        if kind < 2:
            forward(i, kind)
        elif kind == 2:
            product(i)
        elif kind == 3:
            pair_step(i)
        elif kind < 6:
            tree_step(i, kind - 2)
        elif i == 0:
            send_tokens()
        else:
            take_tokens()

    for dz in range(1, N):
        t_copy(dz).wait_send()

    @pl.when(c != t_core)
    def _():
        t_copy(0).wait_send()

    swap_all(lambda d: d.wait_send(), None)

    for i in range(PIECES):
        hops, way, half = piece_of(i)
        for part in range(2):
            for leave in onward_ways(hops, way, half):
                w_copy(hops, leave, part, half).wait_send()
        sib_copy(i).wait_send()
        for u in range(2):
            role = role_of(i, u)

            @pl.when(role != 0)
            def _():
                climb(i, u, role).wait_send()

    for i in range(PIECES):
        result(i)


def body(tokens, up_weight, up_bias):
    return pl.pallas_call(
        kernel,
        out_shape=jax.ShapeDtypeStruct((ROWS, 512), BF16),
        in_specs=[
            pl.BlockSpec(memory_space=pltpu.HBM),
            pl.BlockSpec(memory_space=pltpu.HBM),
            pl.BlockSpec(memory_space=pltpu.VMEM),
        ],
        out_specs=pl.BlockSpec(memory_space=pltpu.VMEM),
        scratch_shapes=[
            pltpu.VMEM((2, 4, ROWS, FEAT), BF16),
            pltpu.VMEM((2, ROWS, 4 * FEAT), BF16),
            pltpu.VMEM((9, 2, 2 * HALF, COLS), BF16),
            pltpu.VMEM((PIECES, ROWS, COLS), F32),
            pltpu.VMEM((PIECES, ROWS, COLS), BF16),
            pltpu.VMEM((PIECES, ROWS, COLS), BF16),
            pltpu.VMEM((PIECES, 2, PART, COLS), BF16),
            pltpu.VMEM((PIECES, 4, 2, PART, COLS), BF16),
            pltpu.SemaphoreType.DMA((N,)),
            pltpu.SemaphoreType.DMA((2, 4)),
            pltpu.SemaphoreType.DMA((2, 2)),
            pltpu.SemaphoreType.DMA((3,)),
            pltpu.SemaphoreType.DMA((9, 2, 2)),
            pltpu.SemaphoreType.DMA((9, 2, 2)),
            pltpu.SemaphoreType.DMA((PIECES,)),
            pltpu.SemaphoreType.DMA((PIECES,)),
            pltpu.SemaphoreType.DMA((PIECES, 2)),
            pltpu.SemaphoreType.DMA((PIECES, 4, 2)),
        ],
        name="up_proj",
        compiler_params=pltpu.CompilerParams(
            collective_id=0, has_side_effects=True, vmem_limit_bytes=40 * 2**20
        ),
    )(tokens, up_weight, up_bias)


def solution(mesh):
    return jax.shard_map(
        body,
        mesh=mesh,
        in_specs=(P("depth", ("py", "px")), P("py", ("px", "depth")), P(("px", "py"))),
        out_specs=P("depth", ("px", "py")),
        check_vma=False,
    )
```

```python
import jax
import jax.numpy as jnp
from jax import lax
from jax.experimental import pallas as pl
from jax.experimental.pallas import tpu as pltpu
from jax.sharding import PartitionSpec as P

MESH = pl.DeviceIdType.MESH
BF16, F32 = jnp.bfloat16, jnp.float32
N = 8
ROWS = 192
PIECES = 16
COLS = 256
HALF = 224
FEAT = 112
PART = 96
STEPS = (
    1, 0, 3, 4, 5, 2, 17, 16, 96, 6, 9, 7, 8, 18, 19, 10, 97, 32, 33, 34,
    12, 35, 20, 36, 21, 50, 13, 23, 22, 37, 39, 38, 48, 49, 51, 52, 11, 53, 14, 55,
    54, 24, 26, 40, 42, 25, 27, 71, 15, 66, 67, 41, 65, 70, 64, 43, 58, 57, 56, 68,
    69, 59, 28, 44, 29, 30, 45, 46, 87, 60, 61, 62, 86, 74, 72, 31, 80, 83, 47, 82,
    73, 81, 75, 84, 63, 76, 77, 78, 85, 88, 89, 79,
)
DEEP = {
    4: (1, -1, 0, 0), 2: (1, -1, 0, 0), 5: (1, 1, 0, 0),
    3: (2, -2, 1, 1), 6: (2, 1, 0, 1), 1: (3, -1, 0, 2), 7: (3, 1, 1, 1),
}
FLAT = {
    4: (1, -1, 0, 0), 2: (1, -1, 0, 0), 5: (1, 1, 0, 0), 7: (1, 1, 2, 0),
    3: (2, -3, 0, 1), 6: (2, 2, 3, 1), 1: (2, -1, 1, 1),
}
DEEP_PIECES = 10


def device(x, core, y, z_hi, z_lo):
    return (z_lo, y * 2 + z_hi, x * 2 + core)


def piece_of(i):
    if i < 2:
        return 0, 0, i
    hops, r = (i - 2) // 4 + 1, (i - 2) % 4
    return hops, r % 2, r if hops == 4 else r // 2


def kernel(
    t_ref, w_ref, b_ref, o_ref,
    t_in, t_cat, w_all, own_part, sib_out, sib_in, y_out, y_in,
    t_send, t_recv, swap_send, local_sem, w_send, w_recv, sib_send, sib_recv, y_send, y_recv,
):
    px, py, depth = lax.axis_index("px"), lax.axis_index("py"), lax.axis_index("depth")
    x, c = depth // 2, depth % 2
    y, zh, zl = py // 2, py % 2, px
    z = zh * 4 + zl
    x_right, x_left = (x + 1) % N, (x + N - 1) % N
    near = jnp.where(c == zh, 1, 0)

    barrier = pltpu.get_barrier_semaphore()

    def greet(target):
        pl.semaphore_signal(barrier, inc=1, device_id=target, device_id_type=MESH)

    greet(device((x + 1) % N, c, y, zh, zl))
    greet(device((x + N - 1) % N, c, y, zh, zl))
    greet(device(x, 1 - c, y, zh, zl))
    greet(device(x, zh, y, 1 - zh, zl))
    for ct in range(2):
        for kz in range(2):
            for b in range(2):
                zl_from = 2 * c + b

                @pl.when((kz != zh) | (zl_from != zl))
                def _(ct=ct, kz=kz, zl_from=zl_from):
                    greet(device(x, ct, y, kz, zl_from))

    for dy in (1, 2, 3, 5, 6, 7):
        greet(device(x, c, (y + dy) % N, zh, zl))
    pl.semaphore_wait(barrier, 3 + 2 * (1 - near) + 7 + 6)

    def swap(h, q, remote):
        src = w_ref.at[pl.ds(h * HALF, HALF), pl.ds(q * COLS, COLS)]
        part = 1 - near
        dst = w_all.at[0, q, pl.ds(pl.multiple_of(part * HALF, HALF), HALF)]
        if remote:
            return pltpu.make_async_remote_copy(
                src_ref=src, dst_ref=dst, send_sem=swap_send.at[h, q], recv_sem=w_recv.at[0, part, q],
                device_id=device(x, h, y, c, zl), device_id_type=MESH)
        return pltpu.make_async_copy(src, dst, local_sem.at[q])

    def swap_all(run_remote, run_local):
        for q in range(2):
            for h in range(2):
                here = (c == zh) & (c == h)
                if run_local is not None:
                    @pl.when(here)
                    def _(h=h, q=q):
                        run_local(swap(h, q, False))

                @pl.when(jnp.logical_not(here))
                def _(h=h, q=q):
                    run_remote(swap(h, q, True))

    t_core = zl // 2
    b_mine = zl % 2

    def t_copy(dz):
        zd = (z + dz) % N
        zhd = zd // 4
        other = jnp.where(c == t_core, 0, 1)
        rel = jnp.where(zhd == zh, 0, 1)
        return pltpu.make_async_remote_copy(
            src_ref=t_ref, dst_ref=t_in.at[other, rel * 2 + b_mine], send_sem=t_send.at[dz],
            recv_sem=t_recv.at[other, rel * 2 + b_mine],
            device_id=device(x, t_core, y, zhd, zd % 4), device_id_type=MESH)

    def t_local():
        return pltpu.make_async_copy(t_ref, t_in.at[0, b_mine], local_sem.at[2])

    def send_tokens():
        for dz in (4, 3, 5, 2, 6, 1, 7):
            t_copy(dz).start()

        @pl.when(c != t_core)
        def _():
            t_copy(0).start()

        @pl.when(c == t_core)
        def _():
            t_local().start()

    swap_all(lambda d: d.start(), lambda d: d.start())

    def w_copy(hops, way, part, half):
        rows = pl.ds(part * HALF, HALF)
        slot = hops + 4 * way if hops else 0
        to = hops + 1 + 4 * way
        return pltpu.make_async_remote_copy(
            src_ref=w_all.at[slot, half, rows], dst_ref=w_all.at[to, half, rows],
            send_sem=w_send.at[to, part, half], recv_sem=w_recv.at[to, part, half],
            device_id=device(x_left if way else x_right, c, y, zh, zl), device_id_type=MESH)

    def w_arrived(slot, part, half):
        ref = w_all.at[slot, half, pl.ds(part * HALF, HALF)]
        pltpu.make_async_copy(ref, ref, w_recv.at[slot, part, half]).wait()

    def onward_ways(hops, way, half):
        if hops == 0:
            return (0, 1)
        return (way,) if hops < 3 or (hops == 3 and half == way) else ()

    def forward(i, part):
        hops, way, half = piece_of(i)
        slot = hops + 4 * way

        if part == 0 and i < 2:
            @pl.when(c == zh)
            def _():
                ref = w_all.at[0, half, pl.ds(0, HALF)]
                pltpu.make_async_copy(ref, ref, local_sem.at[half]).wait()

            @pl.when(c != zh)
            def _():
                w_arrived(slot, 0, half)
        else:
            w_arrived(slot, part, half)
        for leave in onward_ways(hops, way, half):
            w_copy(hops, leave, part, half).start()

    def sib_copy(i):
        return pltpu.make_async_remote_copy(
            src_ref=sib_out.at[i], dst_ref=sib_in.at[i], send_sem=sib_send.at[i], recv_sem=sib_recv.at[i],
            device_id=device(x, 1 - c, y, zh, zl), device_id_type=MESH)

    def product(i):
        hops, way, half = piece_of(i)
        w = w_all[hops + 4 * way, half]
        sib_out[i] = jnp.dot(t_cat[1], w, preferred_element_type=F32).astype(BF16)
        sib_copy(i).start()
        own_part[i] = jnp.dot(t_cat[0], w, preferred_element_type=F32)

    def tree_of(i):
        return DEEP if i < DEEP_PIECES else FLAT

    def climb(i, u, role):
        step, slot = 0, 0
        for r, (_, r_step, r_slot, _) in tree_of(i).items():
            step = jnp.where(role == r, r_step, step)
            slot = jnp.where(role == r, r_slot, slot)
        return pltpu.make_async_remote_copy(
            src_ref=y_out.at[i, u], dst_ref=y_in.at[i, slot, u],
            send_sem=y_send.at[i, u], recv_sem=y_recv.at[i, slot, u],
            device_id=device(x, c, (y + N + step * (1 - 2 * u)) % N, zh, zl), device_id_type=MESH)

    def role_of(i, u):
        hops, way, half = piece_of(i)
        owner = (x + N + hops * (2 * way - 1)) % N
        return (N + (y - owner) * (1 - 2 * u)) % N

    def received(i, k, u):
        ref = y_in.at[i, k, u]
        pltpu.make_async_copy(ref, ref, y_recv.at[i, k, u]).wait()
        return y_in[i, k, u].astype(F32)

    def any_of(role, roles):
        hit = role == roles[0]
        for r in roles[1:]:
            hit = hit | (role == r)
        return hit

    def pair_step(i):
        sib_copy(i).wait_recv()
        leaves = [r for r, v in tree_of(i).items() if v[0] == 1]
        for u in range(2):
            role = role_of(i, u)
            rows = slice(u * PART, (u + 1) * PART)
            value = own_part[i, rows] + sib_in[i, rows].astype(F32)
            leaf = any_of(role, leaves)

            @pl.when(leaf)
            def _():
                y_out[i, u] = value.astype(BF16)
                climb(i, u, role).start()

            @pl.when(jnp.logical_not(leaf))
            def _():
                own_part[i, rows] = value

    def tree_step(i, level):
        for u in range(2):
            role = role_of(i, u)
            rows = slice(u * PART, (u + 1) * PART)
            for count in (1, 2):
                roles = [r for r, v in tree_of(i).items() if v[0] == level and v[3] == count]
                if not roles:
                    continue

                @pl.when(any_of(role, roles))
                def _(count=count):
                    value = own_part[i, rows]
                    for k in range(count):
                        value = value + received(i, k, u)
                    y_out[i, u] = value.astype(BF16)
                    climb(i, u, role).start()

    def result(i):
        _, _, half = piece_of(i)
        cols = slice(half * COLS, (half + 1) * COLS)

        @pl.when(role_of(i, 0) == 0)
        def _():
            for u in range(2):
                rows = slice(u * PART, (u + 1) * PART)
                value = own_part[i, rows]
                for k in range(2 if i < DEEP_PIECES else 4):
                    value = value + received(i, k, u)
                value = value + b_ref[cols].astype(F32)[None, :]
                inner = 0.7978845608028654 * (value + 0.044715 * (value * value * value))
                o_ref[rows, cols] = (0.5 * value * (1.0 + jnp.tanh(inner))).astype(BF16)

    def take_tokens():
        for other in range(2):
            for s in range(4):
                mine = (other == 0) & (s == b_mine) & (c == t_core)

                @pl.when(mine)
                def _():
                    t_local().wait()

                @pl.when(jnp.logical_not(mine))
                def _(other=other, s=s):
                    ref = t_in.at[other, s]
                    pltpu.make_async_copy(ref, ref, t_recv.at[other, s]).wait()

            t_cat[other] = jnp.concatenate([t_in[other, s] for s in range(4)], axis=-1)

    for code in STEPS:
        kind, i = code // 16, code % 16
        if kind < 2:
            forward(i, kind)
        elif kind == 2:
            product(i)
        elif kind == 3:
            pair_step(i)
        elif kind < 6:
            tree_step(i, kind - 2)
        elif i == 0:
            send_tokens()
        else:
            take_tokens()

    for dz in range(1, N):
        t_copy(dz).wait_send()

    @pl.when(c != t_core)
    def _():
        t_copy(0).wait_send()

    swap_all(lambda d: d.wait_send(), None)

    for i in range(PIECES):
        hops, way, half = piece_of(i)
        for part in range(2):
            for leave in onward_ways(hops, way, half):
                w_copy(hops, leave, part, half).wait_send()
        sib_copy(i).wait_send()
        for u in range(2):
            role = role_of(i, u)

            @pl.when(role != 0)
            def _():
                climb(i, u, role).wait_send()

    for i in range(PIECES):
        result(i)


def body(tokens, up_weight, up_bias):
    return pl.pallas_call(
        kernel,
        out_shape=jax.ShapeDtypeStruct((ROWS, 512), BF16),
        in_specs=[
            pl.BlockSpec(memory_space=pltpu.HBM),
            pl.BlockSpec(memory_space=pltpu.HBM),
            pl.BlockSpec(memory_space=pltpu.VMEM),
        ],
        out_specs=pl.BlockSpec(memory_space=pltpu.VMEM),
        scratch_shapes=[
            pltpu.VMEM((2, 4, ROWS, FEAT), BF16),
            pltpu.VMEM((2, ROWS, 4 * FEAT), BF16),
            pltpu.VMEM((9, 2, 2 * HALF, COLS), BF16),
            pltpu.VMEM((PIECES, ROWS, COLS), F32),
            pltpu.VMEM((PIECES, ROWS, COLS), BF16),
            pltpu.VMEM((PIECES, ROWS, COLS), BF16),
            pltpu.VMEM((PIECES, 2, PART, COLS), BF16),
            pltpu.VMEM((PIECES, 4, 2, PART, COLS), BF16),
            pltpu.SemaphoreType.DMA((N,)),
            pltpu.SemaphoreType.DMA((2, 4)),
            pltpu.SemaphoreType.DMA((2, 2)),
            pltpu.SemaphoreType.DMA((3,)),
            pltpu.SemaphoreType.DMA((9, 2, 2)),
            pltpu.SemaphoreType.DMA((9, 2, 2)),
            pltpu.SemaphoreType.DMA((PIECES,)),
            pltpu.SemaphoreType.DMA((PIECES,)),
            pltpu.SemaphoreType.DMA((PIECES, 2)),
            pltpu.SemaphoreType.DMA((PIECES, 4, 2)),
        ],
        name="up_proj",
        compiler_params=pltpu.CompilerParams(
            collective_id=0, has_side_effects=True, vmem_limit_bytes=60 * 2**20
        ),
    )(tokens, up_weight, up_bias)


def solution(mesh):
    return jax.shard_map(
        body,
        mesh=mesh,
        in_specs=(P("depth", ("py", "px")), P("py", ("px", "depth")), P(("px", "py"))),
        out_specs=P("depth", ("px", "py")),
        check_vma=False,
    )
```

```python
import jax
import jax.numpy as jnp
from jax import lax
from jax.experimental import pallas as pl
from jax.experimental.pallas import tpu as pltpu
from jax.sharding import PartitionSpec as P

MESH = pl.DeviceIdType.MESH
BF16, F32 = jnp.bfloat16, jnp.float32
N = 8
ROWS = 192
PIECES = 16
COLS = 256
HALF = 224
FEAT = 112
PART = 96
STEPS = (
    0, 1, 2, 5, 4, 3, 16, 96, 6, 17, 9, 18, 8, 7, 10, 19, 97, 34, 20, 35,
    21, 11, 33, 32, 12, 37, 36, 23, 51, 22, 49, 38, 53, 50, 48, 13, 52, 39, 54, 24,
    55, 40, 25, 26, 42, 56, 41, 67, 27, 43, 66, 71, 15, 14, 70, 57, 58, 64, 65, 28,
    59, 44, 29, 30, 45, 46, 60, 68, 61, 62, 86, 75, 72, 87, 31, 47, 74, 73, 63, 76,
    84, 69, 77, 78, 88, 83, 80, 89, 85, 79, 82, 81,
)
DEEP = {
    4: (1, -1, 0, 0), 2: (1, -1, 0, 0), 5: (1, 1, 0, 0),
    3: (2, -2, 1, 1), 6: (2, 1, 0, 1), 1: (3, -1, 0, 2), 7: (3, 1, 1, 1),
}
FLAT = {
    4: (1, -1, 0, 0), 2: (1, -1, 0, 0), 5: (1, 1, 0, 0), 7: (1, 1, 2, 0),
    3: (2, -3, 0, 1), 6: (2, 2, 3, 1), 1: (2, -1, 1, 1),
}
DEEP_PIECES = 10


def device(x, core, y, z_hi, z_lo):
    return (z_lo, y * 2 + z_hi, x * 2 + core)


def piece_of(i):
    if i < 2:
        return 0, 0, i
    hops, r = (i - 2) // 4 + 1, (i - 2) % 4
    return hops, r % 2, r if hops == 4 else r // 2


def kernel(
    t_ref, w_ref, b_ref, o_ref,
    t_in, t_cat, w_all, own_part, sib_out, sib_in, y_out, y_in,
    t_send, t_recv, swap_send, local_sem, w_send, w_recv, sib_send, sib_recv, y_send, y_recv,
):
    px, py, depth = lax.axis_index("px"), lax.axis_index("py"), lax.axis_index("depth")
    x, c = depth // 2, depth % 2
    y, zh, zl = py // 2, py % 2, px
    z = zh * 4 + zl
    x_right, x_left = (x + 1) % N, (x + N - 1) % N
    near = jnp.where(c == zh, 1, 0)

    barrier = pltpu.get_barrier_semaphore()

    def greet(target):
        pl.semaphore_signal(barrier, inc=1, device_id=target, device_id_type=MESH)

    greet(device((x + 1) % N, c, y, zh, zl))
    greet(device((x + N - 1) % N, c, y, zh, zl))
    greet(device(x, 1 - c, y, zh, zl))
    greet(device(x, zh, y, 1 - zh, zl))
    for ct in range(2):
        for kz in range(2):
            for b in range(2):
                zl_from = 2 * c + b

                @pl.when((kz != zh) | (zl_from != zl))
                def _(ct=ct, kz=kz, zl_from=zl_from):
                    greet(device(x, ct, y, kz, zl_from))

    for dy in (1, 2, 3, 5, 6, 7):
        greet(device(x, c, (y + dy) % N, zh, zl))
    pl.semaphore_wait(barrier, 3 + 2 * (1 - near) + 7 + 6)

    def swap(h, q, remote):
        src = w_ref.at[pl.ds(h * HALF, HALF), pl.ds(q * COLS, COLS)]
        part = 1 - near
        dst = w_all.at[0, q, pl.ds(pl.multiple_of(part * HALF, HALF), HALF)]
        if remote:
            return pltpu.make_async_remote_copy(
                src_ref=src, dst_ref=dst, send_sem=swap_send.at[h, q], recv_sem=w_recv.at[0, part, q],
                device_id=device(x, h, y, c, zl), device_id_type=MESH)
        return pltpu.make_async_copy(src, dst, local_sem.at[q])

    def swap_all(run_remote, run_local):
        for q in range(2):
            for h in range(2):
                here = (c == zh) & (c == h)
                if run_local is not None:
                    @pl.when(here)
                    def _(h=h, q=q):
                        run_local(swap(h, q, False))

                @pl.when(jnp.logical_not(here))
                def _(h=h, q=q):
                    run_remote(swap(h, q, True))

    t_core = zl // 2
    b_mine = zl % 2

    def t_copy(dz):
        zd = (z + dz) % N
        zhd = zd // 4
        other = jnp.where(c == t_core, 0, 1)
        rel = jnp.where(zhd == zh, 0, 1)
        return pltpu.make_async_remote_copy(
            src_ref=t_ref, dst_ref=t_in.at[other, rel * 2 + b_mine], send_sem=t_send.at[dz],
            recv_sem=t_recv.at[other, rel * 2 + b_mine],
            device_id=device(x, t_core, y, zhd, zd % 4), device_id_type=MESH)

    def t_local():
        return pltpu.make_async_copy(t_ref, t_in.at[0, b_mine], local_sem.at[2])

    def send_tokens():
        for dz in (4, 3, 5, 2, 6, 1, 7):
            t_copy(dz).start()

        @pl.when(c != t_core)
        def _():
            t_copy(0).start()

        @pl.when(c == t_core)
        def _():
            t_local().start()

    swap_all(lambda d: d.start(), lambda d: d.start())

    def w_copy(hops, way, part, half):
        rows = pl.ds(part * HALF, HALF)
        slot = hops + 4 * way if hops else 0
        to = hops + 1 + 4 * way
        return pltpu.make_async_remote_copy(
            src_ref=w_all.at[slot, half, rows], dst_ref=w_all.at[to, half, rows],
            send_sem=w_send.at[to, part, half], recv_sem=w_recv.at[to, part, half],
            device_id=device(x_left if way else x_right, c, y, zh, zl), device_id_type=MESH)

    def w_arrived(slot, part, half):
        ref = w_all.at[slot, half, pl.ds(part * HALF, HALF)]
        pltpu.make_async_copy(ref, ref, w_recv.at[slot, part, half]).wait()

    def onward_ways(hops, way, half):
        if hops == 0:
            return (0, 1)
        return (way,) if hops < 3 or (hops == 3 and half == way) else ()

    def forward(i, part):
        hops, way, half = piece_of(i)
        slot = hops + 4 * way

        if part == 0 and i < 2:
            @pl.when(c == zh)
            def _():
                ref = w_all.at[0, half, pl.ds(0, HALF)]
                pltpu.make_async_copy(ref, ref, local_sem.at[half]).wait()

            @pl.when(c != zh)
            def _():
                w_arrived(slot, 0, half)
        else:
            w_arrived(slot, part, half)
        for leave in onward_ways(hops, way, half):
            w_copy(hops, leave, part, half).start()

    def sib_copy(i):
        return pltpu.make_async_remote_copy(
            src_ref=sib_out.at[i], dst_ref=sib_in.at[i], send_sem=sib_send.at[i], recv_sem=sib_recv.at[i],
            device_id=device(x, 1 - c, y, zh, zl), device_id_type=MESH)

    def product(i):
        hops, way, half = piece_of(i)
        w = w_all[hops + 4 * way, half]
        sib_out[i] = jnp.dot(t_cat[1], w, preferred_element_type=F32).astype(BF16)
        sib_copy(i).start()
        own_part[i] = jnp.dot(t_cat[0], w, preferred_element_type=F32)

    def tree_of(i):
        return DEEP if i < DEEP_PIECES else FLAT

    def climb(i, u, role):
        step, slot = 0, 0
        for r, (_, r_step, r_slot, _) in tree_of(i).items():
            step = jnp.where(role == r, r_step, step)
            slot = jnp.where(role == r, r_slot, slot)
        return pltpu.make_async_remote_copy(
            src_ref=y_out.at[i, u], dst_ref=y_in.at[i, slot, u],
            send_sem=y_send.at[i, u], recv_sem=y_recv.at[i, slot, u],
            device_id=device(x, c, (y + N + step * (1 - 2 * u)) % N, zh, zl), device_id_type=MESH)

    def role_of(i, u):
        hops, way, half = piece_of(i)
        owner = (x + N + hops * (2 * way - 1)) % N
        return (N + (y - owner) * (1 - 2 * u)) % N

    def received(i, k, u):
        ref = y_in.at[i, k, u]
        pltpu.make_async_copy(ref, ref, y_recv.at[i, k, u]).wait()
        return y_in[i, k, u].astype(F32)

    def any_of(role, roles):
        hit = role == roles[0]
        for r in roles[1:]:
            hit = hit | (role == r)
        return hit

    def pair_step(i):
        sib_copy(i).wait_recv()
        leaves = [r for r, v in tree_of(i).items() if v[0] == 1]
        for u in range(2):
            role = role_of(i, u)
            rows = slice(u * PART, (u + 1) * PART)
            value = own_part[i, rows] + sib_in[i, rows].astype(F32)
            leaf = any_of(role, leaves)

            @pl.when(leaf)
            def _():
                y_out[i, u] = value.astype(BF16)
                climb(i, u, role).start()

            @pl.when(jnp.logical_not(leaf))
            def _():
                own_part[i, rows] = value

    def tree_step(i, level):
        for u in range(2):
            role = role_of(i, u)
            rows = slice(u * PART, (u + 1) * PART)
            for count in (1, 2):
                roles = [r for r, v in tree_of(i).items() if v[0] == level and v[3] == count]
                if not roles:
                    continue

                @pl.when(any_of(role, roles))
                def _(count=count):
                    value = own_part[i, rows]
                    for k in range(count):
                        value = value + received(i, k, u)
                    y_out[i, u] = value.astype(BF16)
                    climb(i, u, role).start()

    def result(i):
        _, _, half = piece_of(i)
        cols = slice(half * COLS, (half + 1) * COLS)

        @pl.when(role_of(i, 0) == 0)
        def _():
            for u in range(2):
                rows = slice(u * PART, (u + 1) * PART)
                value = own_part[i, rows]
                for k in range(2 if i < DEEP_PIECES else 4):
                    value = value + received(i, k, u)
                value = value + b_ref[cols].astype(F32)[None, :]
                inner = 0.7978845608028654 * (value + 0.044715 * (value * value * value))
                o_ref[rows, cols] = (0.5 * value * (1.0 + jnp.tanh(inner))).astype(BF16)

    def take_tokens():
        for other in range(2):
            for s in range(4):
                mine = (other == 0) & (s == b_mine) & (c == t_core)

                @pl.when(mine)
                def _():
                    t_local().wait()

                @pl.when(jnp.logical_not(mine))
                def _(other=other, s=s):
                    ref = t_in.at[other, s]
                    pltpu.make_async_copy(ref, ref, t_recv.at[other, s]).wait()

            t_cat[other] = jnp.concatenate([t_in[other, s] for s in range(4)], axis=-1)

    for code in STEPS:
        kind, i = code // 16, code % 16
        if kind < 2:
            forward(i, kind)
        elif kind == 2:
            product(i)
        elif kind == 3:
            pair_step(i)
        elif kind < 6:
            tree_step(i, kind - 2)
        elif i == 0:
            send_tokens()
        else:
            take_tokens()

    for dz in range(1, N):
        t_copy(dz).wait_send()

    @pl.when(c != t_core)
    def _():
        t_copy(0).wait_send()

    swap_all(lambda d: d.wait_send(), None)

    for i in range(PIECES):
        hops, way, half = piece_of(i)
        for part in range(2):
            for leave in onward_ways(hops, way, half):
                w_copy(hops, leave, part, half).wait_send()
        sib_copy(i).wait_send()
        for u in range(2):
            role = role_of(i, u)

            @pl.when(role != 0)
            def _():
                climb(i, u, role).wait_send()

    for i in range(PIECES):
        result(i)


def body(tokens, up_weight, up_bias):
    return pl.pallas_call(
        kernel,
        out_shape=jax.ShapeDtypeStruct((ROWS, 512), BF16),
        in_specs=[
            pl.BlockSpec(memory_space=pltpu.HBM),
            pl.BlockSpec(memory_space=pltpu.HBM),
            pl.BlockSpec(memory_space=pltpu.VMEM),
        ],
        out_specs=pl.BlockSpec(memory_space=pltpu.VMEM),
        scratch_shapes=[
            pltpu.VMEM((2, 4, ROWS, FEAT), BF16),
            pltpu.VMEM((2, ROWS, 4 * FEAT), BF16),
            pltpu.VMEM((9, 2, 2 * HALF, COLS), BF16),
            pltpu.VMEM((PIECES, ROWS, COLS), F32),
            pltpu.VMEM((PIECES, ROWS, COLS), BF16),
            pltpu.VMEM((PIECES, ROWS, COLS), BF16),
            pltpu.VMEM((PIECES, 2, PART, COLS), BF16),
            pltpu.VMEM((PIECES, 4, 2, PART, COLS), BF16),
            pltpu.SemaphoreType.DMA((N,)),
            pltpu.SemaphoreType.DMA((2, 4)),
            pltpu.SemaphoreType.DMA((2, 2)),
            pltpu.SemaphoreType.DMA((3,)),
            pltpu.SemaphoreType.DMA((9, 2, 2)),
            pltpu.SemaphoreType.DMA((9, 2, 2)),
            pltpu.SemaphoreType.DMA((PIECES,)),
            pltpu.SemaphoreType.DMA((PIECES,)),
            pltpu.SemaphoreType.DMA((PIECES, 2)),
            pltpu.SemaphoreType.DMA((PIECES, 4, 2)),
        ],
        name="up_proj",
        compiler_params=pltpu.CompilerParams(
            collective_id=0, has_side_effects=True, vmem_limit_bytes=60 * 2**20
        ),
    )(tokens, up_weight, up_bias)


def solution(mesh):
    return jax.shard_map(
        body,
        mesh=mesh,
        in_specs=(P("depth", ("py", "px")), P("py", ("px", "depth")), P(("px", "py"))),
        out_specs=P("depth", ("px", "py")),
        check_vma=False,
    )
```

```python
import jax
import jax.numpy as jnp
from jax import lax
from jax.experimental import pallas as pl
from jax.experimental.pallas import tpu as pltpu
from jax.sharding import PartitionSpec as P

MESH = pl.DeviceIdType.MESH
BF16, F32 = jnp.bfloat16, jnp.float32
N = 8
ROWS = 192
PIECES = 16
COLS = 256
HALF = 224
FEAT = 112
PART = 96
STEPS = (
    0, 1, 98, 2, 5, 4, 3, 16, 96, 6, 17, 9, 18, 8, 7, 10, 19, 97, 34, 20, 35,
    21, 11, 33, 32, 12, 37, 36, 23, 51, 22, 49, 38, 53, 50, 48, 13, 52, 39, 54, 24,
    55, 40, 25, 26, 42, 56, 41, 67, 27, 43, 66, 71, 15, 14, 70, 57, 58, 64, 65, 28,
    59, 44, 29, 30, 45, 46, 60, 68, 61, 62, 86, 75, 72, 87, 31, 47, 74, 73, 63, 76,
    84, 69, 77, 78, 88, 83, 80, 89, 85, 79, 82, 81,
)
DEEP = {
    4: (1, -1, 0, 0), 2: (1, -1, 0, 0), 5: (1, 1, 0, 0),
    3: (2, -2, 1, 1), 6: (2, 1, 0, 1), 1: (3, -1, 0, 2), 7: (3, 1, 1, 1),
}
FLAT = {
    4: (1, -1, 0, 0), 2: (1, -1, 0, 0), 5: (1, 1, 0, 0), 7: (1, 1, 2, 0),
    3: (2, -3, 0, 1), 6: (2, 2, 3, 1), 1: (2, -1, 1, 1),
}
DEEP_PIECES = 10


def device(x, core, y, z_hi, z_lo):
    return (z_lo, y * 2 + z_hi, x * 2 + core)


def piece_of(i):
    if i < 2:
        return 0, 0, i
    hops, r = (i - 2) // 4 + 1, (i - 2) % 4
    return hops, r % 2, r if hops == 4 else r // 2


def kernel(
    t_ref, w_ref, b_ref, o_ref,
    t_in, t_cat, w_all, own_part, sib_out, sib_in, y_out, y_in,
    t_send, t_recv, swap_send, local_sem, w_send, w_recv, sib_send, sib_recv, y_send, y_recv,
):
    px, py, depth = lax.axis_index("px"), lax.axis_index("py"), lax.axis_index("depth")
    x, c = depth // 2, depth % 2
    y, zh, zl = py // 2, py % 2, px
    z = zh * 4 + zl
    x_right, x_left = (x + 1) % N, (x + N - 1) % N
    near = jnp.where(c == zh, 1, 0)

    barrier = pltpu.get_barrier_semaphore()

    def greet(target):
        pl.semaphore_signal(barrier, inc=1, device_id=target, device_id_type=MESH)

    greet(device((x + 1) % N, c, y, zh, zl))
    greet(device((x + N - 1) % N, c, y, zh, zl))
    greet(device(x, 1 - c, y, zh, zl))
    greet(device(x, zh, y, 1 - zh, zl))
    for ct in range(2):
        for kz in range(2):
            for b in range(2):
                zl_from = 2 * c + b

                @pl.when((kz != zh) | (zl_from != zl))
                def _(ct=ct, kz=kz, zl_from=zl_from):
                    greet(device(x, ct, y, kz, zl_from))

    for dy in (1, 2, 3, 5, 6, 7):
        greet(device(x, c, (y + dy) % N, zh, zl))
    pl.semaphore_wait(barrier, 3 + 2 * (1 - near) + 7 + 6)

    def swap(h, q, remote):
        src = w_ref.at[pl.ds(h * HALF, HALF), pl.ds(q * COLS, COLS)]
        part = 1 - near
        dst = w_all.at[0, q, pl.ds(pl.multiple_of(part * HALF, HALF), HALF)]
        if remote:
            return pltpu.make_async_remote_copy(
                src_ref=src, dst_ref=dst, send_sem=swap_send.at[h, q], recv_sem=w_recv.at[0, part, q],
                device_id=device(x, h, y, c, zl), device_id_type=MESH)
        return pltpu.make_async_copy(src, dst, local_sem.at[q])

    def swap_all(run_remote, run_local, halves=(0, 1)):
        for q in halves:
            for h in range(2):
                here = (c == zh) & (c == h)
                if run_local is not None:
                    @pl.when(here)
                    def _(h=h, q=q):
                        run_local(swap(h, q, False))

                @pl.when(jnp.logical_not(here))
                def _(h=h, q=q):
                    run_remote(swap(h, q, True))

    t_core = zl // 2
    b_mine = zl % 2

    def t_copy(dz):
        zd = (z + dz) % N
        zhd = zd // 4
        other = jnp.where(c == t_core, 0, 1)
        rel = jnp.where(zhd == zh, 0, 1)
        return pltpu.make_async_remote_copy(
            src_ref=t_ref, dst_ref=t_in.at[other, rel * 2 + b_mine], send_sem=t_send.at[dz],
            recv_sem=t_recv.at[other, rel * 2 + b_mine],
            device_id=device(x, t_core, y, zhd, zd % 4), device_id_type=MESH)

    def t_local():
        return pltpu.make_async_copy(t_ref, t_in.at[0, b_mine], local_sem.at[2])

    def send_tokens():
        for dz in (4, 3, 5, 2, 6, 1, 7):
            t_copy(dz).start()

        @pl.when(c != t_core)
        def _():
            t_copy(0).start()

        @pl.when(c == t_core)
        def _():
            t_local().start()

    swap_all(lambda d: d.start(), lambda d: d.start(), (0,))

    @pl.when(c == zh)
    def _():
        swap_all(lambda d: d.start(), lambda d: d.start(), (1,))

    def swap_second_half():
        @pl.when(c != zh)
        def _():
            swap_all(lambda d: d.wait_send(), None, (0,))
            swap_all(lambda d: d.start(), None, (1,))

    def w_copy(hops, way, part, half):
        rows = pl.ds(part * HALF, HALF)
        slot = hops + 4 * way if hops else 0
        to = hops + 1 + 4 * way
        return pltpu.make_async_remote_copy(
            src_ref=w_all.at[slot, half, rows], dst_ref=w_all.at[to, half, rows],
            send_sem=w_send.at[to, part, half], recv_sem=w_recv.at[to, part, half],
            device_id=device(x_left if way else x_right, c, y, zh, zl), device_id_type=MESH)

    def w_arrived(slot, part, half):
        ref = w_all.at[slot, half, pl.ds(part * HALF, HALF)]
        pltpu.make_async_copy(ref, ref, w_recv.at[slot, part, half]).wait()

    def onward_ways(hops, way, half):
        if hops == 0:
            return (0, 1)
        return (way,) if hops < 3 or (hops == 3 and half == way) else ()

    def forward(i, part):
        hops, way, half = piece_of(i)
        slot = hops + 4 * way

        if part == 0 and i < 2:
            @pl.when(c == zh)
            def _():
                ref = w_all.at[0, half, pl.ds(0, HALF)]
                pltpu.make_async_copy(ref, ref, local_sem.at[half]).wait()

            @pl.when(c != zh)
            def _():
                w_arrived(slot, 0, half)
        else:
            w_arrived(slot, part, half)
        for leave in onward_ways(hops, way, half):
            w_copy(hops, leave, part, half).start()

    def sib_copy(i):
        return pltpu.make_async_remote_copy(
            src_ref=sib_out.at[i], dst_ref=sib_in.at[i], send_sem=sib_send.at[i], recv_sem=sib_recv.at[i],
            device_id=device(x, 1 - c, y, zh, zl), device_id_type=MESH)

    def product(i):
        hops, way, half = piece_of(i)
        w = w_all[hops + 4 * way, half]
        sib_out[i] = jnp.dot(t_cat[1], w, preferred_element_type=F32).astype(BF16)
        sib_copy(i).start()
        own_part[i] = jnp.dot(t_cat[0], w, preferred_element_type=F32)

    def tree_of(i):
        return DEEP if i < DEEP_PIECES else FLAT

    def climb(i, u, role):
        step, slot = 0, 0
        for r, (_, r_step, r_slot, _) in tree_of(i).items():
            step = jnp.where(role == r, r_step, step)
            slot = jnp.where(role == r, r_slot, slot)
        return pltpu.make_async_remote_copy(
            src_ref=y_out.at[i, u], dst_ref=y_in.at[i, slot, u],
            send_sem=y_send.at[i, u], recv_sem=y_recv.at[i, slot, u],
            device_id=device(x, c, (y + N + step * (1 - 2 * u)) % N, zh, zl), device_id_type=MESH)

    def role_of(i, u):
        hops, way, half = piece_of(i)
        owner = (x + N + hops * (2 * way - 1)) % N
        return (N + (y - owner) * (1 - 2 * u)) % N

    def received(i, k, u):
        ref = y_in.at[i, k, u]
        pltpu.make_async_copy(ref, ref, y_recv.at[i, k, u]).wait()
        return y_in[i, k, u].astype(F32)

    def any_of(role, roles):
        hit = role == roles[0]
        for r in roles[1:]:
            hit = hit | (role == r)
        return hit

    def pair_step(i):
        sib_copy(i).wait_recv()
        leaves = [r for r, v in tree_of(i).items() if v[0] == 1]
        for u in range(2):
            role = role_of(i, u)
            rows = slice(u * PART, (u + 1) * PART)
            value = own_part[i, rows] + sib_in[i, rows].astype(F32)
            leaf = any_of(role, leaves)

            @pl.when(leaf)
            def _():
                y_out[i, u] = value.astype(BF16)
                climb(i, u, role).start()

            @pl.when(jnp.logical_not(leaf))
            def _():
                own_part[i, rows] = value

    def tree_step(i, level):
        for u in range(2):
            role = role_of(i, u)
            rows = slice(u * PART, (u + 1) * PART)
            for count in (1, 2):
                roles = [r for r, v in tree_of(i).items() if v[0] == level and v[3] == count]
                if not roles:
                    continue

                @pl.when(any_of(role, roles))
                def _(count=count):
                    value = own_part[i, rows]
                    for k in range(count):
                        value = value + received(i, k, u)
                    y_out[i, u] = value.astype(BF16)
                    climb(i, u, role).start()

    def result(i):
        _, _, half = piece_of(i)
        cols = slice(half * COLS, (half + 1) * COLS)

        @pl.when(role_of(i, 0) == 0)
        def _():
            for u in range(2):
                rows = slice(u * PART, (u + 1) * PART)
                value = own_part[i, rows]
                for k in range(2 if i < DEEP_PIECES else 4):
                    value = value + received(i, k, u)
                value = value + b_ref[cols].astype(F32)[None, :]
                inner = 0.7978845608028654 * (value + 0.044715 * (value * value * value))
                o_ref[rows, cols] = (0.5 * value * (1.0 + jnp.tanh(inner))).astype(BF16)

    def take_tokens():
        for other in range(2):
            for s in range(4):
                mine = (other == 0) & (s == b_mine) & (c == t_core)

                @pl.when(mine)
                def _():
                    t_local().wait()

                @pl.when(jnp.logical_not(mine))
                def _(other=other, s=s):
                    ref = t_in.at[other, s]
                    pltpu.make_async_copy(ref, ref, t_recv.at[other, s]).wait()

            t_cat[other] = jnp.concatenate([t_in[other, s] for s in range(4)], axis=-1)

    for code in STEPS:
        kind, i = code // 16, code % 16
        if kind < 2:
            forward(i, kind)
        elif kind == 2:
            product(i)
        elif kind == 3:
            pair_step(i)
        elif kind < 6:
            tree_step(i, kind - 2)
        elif i == 0:
            send_tokens()
        elif i == 2:
            swap_second_half()
        else:
            take_tokens()

    for dz in range(1, N):
        t_copy(dz).wait_send()

    @pl.when(c != t_core)
    def _():
        t_copy(0).wait_send()

    swap_all(lambda d: d.wait_send(), None, (1,))

    @pl.when(c == zh)
    def _():
        swap_all(lambda d: d.wait_send(), None, (0,))

    for i in range(PIECES):
        hops, way, half = piece_of(i)
        for part in range(2):
            for leave in onward_ways(hops, way, half):
                w_copy(hops, leave, part, half).wait_send()
        sib_copy(i).wait_send()
        for u in range(2):
            role = role_of(i, u)

            @pl.when(role != 0)
            def _():
                climb(i, u, role).wait_send()

    for i in range(PIECES):
        result(i)


def body(tokens, up_weight, up_bias):
    return pl.pallas_call(
        kernel,
        out_shape=jax.ShapeDtypeStruct((ROWS, 512), BF16),
        in_specs=[
            pl.BlockSpec(memory_space=pltpu.HBM),
            pl.BlockSpec(memory_space=pltpu.HBM),
            pl.BlockSpec(memory_space=pltpu.VMEM),
        ],
        out_specs=pl.BlockSpec(memory_space=pltpu.VMEM),
        scratch_shapes=[
            pltpu.VMEM((2, 4, ROWS, FEAT), BF16),
            pltpu.VMEM((2, ROWS, 4 * FEAT), BF16),
            pltpu.VMEM((9, 2, 2 * HALF, COLS), BF16),
            pltpu.VMEM((PIECES, ROWS, COLS), F32),
            pltpu.VMEM((PIECES, ROWS, COLS), BF16),
            pltpu.VMEM((PIECES, ROWS, COLS), BF16),
            pltpu.VMEM((PIECES, 2, PART, COLS), BF16),
            pltpu.VMEM((PIECES, 4, 2, PART, COLS), BF16),
            pltpu.SemaphoreType.DMA((N,)),
            pltpu.SemaphoreType.DMA((2, 4)),
            pltpu.SemaphoreType.DMA((2, 2)),
            pltpu.SemaphoreType.DMA((3,)),
            pltpu.SemaphoreType.DMA((9, 2, 2)),
            pltpu.SemaphoreType.DMA((9, 2, 2)),
            pltpu.SemaphoreType.DMA((PIECES,)),
            pltpu.SemaphoreType.DMA((PIECES,)),
            pltpu.SemaphoreType.DMA((PIECES, 2)),
            pltpu.SemaphoreType.DMA((PIECES, 4, 2)),
        ],
        name="up_proj",
        compiler_params=pltpu.CompilerParams(
            collective_id=0, has_side_effects=True, vmem_limit_bytes=60 * 2**20
        ),
    )(tokens, up_weight, up_bias)


def solution(mesh):
    return jax.shard_map(
        body,
        mesh=mesh,
        in_specs=(P("depth", ("py", "px")), P("py", ("px", "depth")), P(("px", "py"))),
        out_specs=P("depth", ("px", "py")),
        check_vma=False,
    )
```

```python
import jax
import jax.numpy as jnp
from jax import lax
from jax.experimental import pallas as pl
from jax.experimental.pallas import tpu as pltpu
from jax.sharding import PartitionSpec as P

MESH = pl.DeviceIdType.MESH
BF16, F32 = jnp.bfloat16, jnp.float32
N = 8
ROWS = 192
PIECES = 16
COLS = 256
HALF = 224
FEAT = 112
PART = 96
STEPS = (
    0, 1, 2, 5, 4, 3, 16, 96, 6, 17, 9, 18, 8, 7, 10, 19, 97, 34, 20, 35,
    21, 11, 33, 32, 12, 37, 36, 23, 51, 22, 49, 38, 53, 50, 48, 13, 52, 39, 54, 24,
    55, 40, 25, 26, 42, 56, 41, 27, 43, 15, 14, 67, 57, 58, 66, 71, 28, 59, 44, 70,
    29, 30, 45, 64, 46, 65, 60, 61, 62, 31, 68, 47, 63, 75, 72, 86, 74, 73, 87, 76,
    69, 77, 78, 84, 79, 88, 83, 80, 89, 85, 82, 81,
)
DEEP = {
    4: (1, -1, 0, 0), 2: (1, -1, 0, 0), 5: (1, 1, 0, 0),
    3: (2, -2, 1, 1), 6: (2, 1, 0, 1), 1: (3, -1, 0, 2), 7: (3, 1, 1, 1),
}
FLAT = {
    4: (1, -1, 0, 0), 2: (1, -1, 0, 0), 5: (1, 1, 0, 0), 7: (1, 1, 2, 0),
    3: (2, -3, 0, 1), 6: (2, 2, 3, 1), 1: (2, -1, 1, 1),
}
DEEP_PIECES = 10


def device(x, core, y, z_hi, z_lo):
    return (z_lo, y * 2 + z_hi, x * 2 + core)


def piece_of(i):
    if i < 2:
        return 0, 0, i
    hops, r = (i - 2) // 4 + 1, (i - 2) % 4
    return hops, r % 2, r if hops == 4 else r // 2


def kernel(
    t_ref, w_ref, b_ref, o_ref,
    t_in, t_cat, w_all, own_part, sib_out, sib_in, y_out, y_in,
    t_send, t_recv, swap_send, local_sem, w_send, w_recv, sib_send, sib_recv, y_send, y_recv,
):
    px, py, depth = lax.axis_index("px"), lax.axis_index("py"), lax.axis_index("depth")
    x, c = depth // 2, depth % 2
    y, zh, zl = py // 2, py % 2, px
    z = zh * 4 + zl
    x_right, x_left = (x + 1) % N, (x + N - 1) % N
    near = jnp.where(c == zh, 1, 0)

    barrier = pltpu.get_barrier_semaphore()

    def greet(target):
        pl.semaphore_signal(barrier, inc=1, device_id=target, device_id_type=MESH)

    greet(device((x + 1) % N, c, y, zh, zl))
    greet(device((x + N - 1) % N, c, y, zh, zl))
    greet(device(x, 1 - c, y, zh, zl))
    greet(device(x, zh, y, 1 - zh, zl))
    for ct in range(2):
        for kz in range(2):
            for b in range(2):
                zl_from = 2 * c + b

                @pl.when((kz != zh) | (zl_from != zl))
                def _(ct=ct, kz=kz, zl_from=zl_from):
                    greet(device(x, ct, y, kz, zl_from))

    for dy in (1, 2, 3, 5, 6, 7):
        greet(device(x, c, (y + dy) % N, zh, zl))
    pl.semaphore_wait(barrier, 3 + 2 * (1 - near) + 7 + 6)

    def swap(h, q, remote):
        src = w_ref.at[pl.ds(h * HALF, HALF), pl.ds(q * COLS, COLS)]
        part = 1 - near
        dst = w_all.at[0, q, pl.ds(pl.multiple_of(part * HALF, HALF), HALF)]
        if remote:
            return pltpu.make_async_remote_copy(
                src_ref=src, dst_ref=dst, send_sem=swap_send.at[h, q], recv_sem=w_recv.at[0, part, q],
                device_id=device(x, h, y, c, zl), device_id_type=MESH)
        return pltpu.make_async_copy(src, dst, local_sem.at[q])

    def swap_all(run_remote, run_local):
        for q in range(2):
            for h in range(2):
                here = (c == zh) & (c == h)
                if run_local is not None:
                    @pl.when(here)
                    def _(h=h, q=q):
                        run_local(swap(h, q, False))

                @pl.when(jnp.logical_not(here))
                def _(h=h, q=q):
                    run_remote(swap(h, q, True))

    t_core = zl // 2
    b_mine = zl % 2

    def t_copy(dz):
        zd = (z + dz) % N
        zhd = zd // 4
        other = jnp.where(c == t_core, 0, 1)
        rel = jnp.where(zhd == zh, 0, 1)
        return pltpu.make_async_remote_copy(
            src_ref=t_ref, dst_ref=t_in.at[other, rel * 2 + b_mine], send_sem=t_send.at[dz],
            recv_sem=t_recv.at[other, rel * 2 + b_mine],
            device_id=device(x, t_core, y, zhd, zd % 4), device_id_type=MESH)

    def t_local():
        return pltpu.make_async_copy(t_ref, t_in.at[0, b_mine], local_sem.at[2])

    def send_tokens():
        for dz in (4, 3, 5, 2, 6, 1, 7):
            t_copy(dz).start()

        @pl.when(c != t_core)
        def _():
            t_copy(0).start()

        @pl.when(c == t_core)
        def _():
            t_local().start()

    swap_all(lambda d: d.start(), lambda d: d.start())

    def w_copy(hops, way, part, half):
        rows = pl.ds(part * HALF, HALF)
        slot = hops + 4 * way if hops else 0
        to = hops + 1 + 4 * way
        return pltpu.make_async_remote_copy(
            src_ref=w_all.at[slot, half, rows], dst_ref=w_all.at[to, half, rows],
            send_sem=w_send.at[to, part, half], recv_sem=w_recv.at[to, part, half],
            device_id=device(x_left if way else x_right, c, y, zh, zl), device_id_type=MESH)

    def w_arrived(slot, part, half):
        ref = w_all.at[slot, half, pl.ds(part * HALF, HALF)]
        pltpu.make_async_copy(ref, ref, w_recv.at[slot, part, half]).wait()

    def onward_ways(hops, way, half):
        if hops == 0:
            return (0, 1)
        return (way,) if hops < 3 or (hops == 3 and half == way) else ()

    def forward(i, part):
        hops, way, half = piece_of(i)
        slot = hops + 4 * way

        if part == 0 and i < 2:
            @pl.when(c == zh)
            def _():
                ref = w_all.at[0, half, pl.ds(0, HALF)]
                pltpu.make_async_copy(ref, ref, local_sem.at[half]).wait()

            @pl.when(c != zh)
            def _():
                w_arrived(slot, 0, half)
        else:
            w_arrived(slot, part, half)
        for leave in onward_ways(hops, way, half):
            w_copy(hops, leave, part, half).start()

    def sib_copy(i):
        return pltpu.make_async_remote_copy(
            src_ref=sib_out.at[i], dst_ref=sib_in.at[i], send_sem=sib_send.at[i], recv_sem=sib_recv.at[i],
            device_id=device(x, 1 - c, y, zh, zl), device_id_type=MESH)

    def product(i):
        hops, way, half = piece_of(i)
        w = w_all[hops + 4 * way, half]
        sib_out[i] = jnp.dot(t_cat[1], w, preferred_element_type=F32).astype(BF16)
        sib_copy(i).start()
        own_part[i] = jnp.dot(t_cat[0], w, preferred_element_type=F32)

    def tree_of(i):
        return DEEP if i < DEEP_PIECES else FLAT

    def climb(i, u, role):
        step, slot = 0, 0
        for r, (_, r_step, r_slot, _) in tree_of(i).items():
            step = jnp.where(role == r, r_step, step)
            slot = jnp.where(role == r, r_slot, slot)
        return pltpu.make_async_remote_copy(
            src_ref=y_out.at[i, u], dst_ref=y_in.at[i, slot, u],
            send_sem=y_send.at[i, u], recv_sem=y_recv.at[i, slot, u],
            device_id=device(x, c, (y + N + step * (1 - 2 * u)) % N, zh, zl), device_id_type=MESH)

    def role_of(i, u):
        hops, way, half = piece_of(i)
        owner = (x + N + hops * (2 * way - 1)) % N
        return (N + (y - owner) * (1 - 2 * u)) % N

    def received(i, k, u):
        ref = y_in.at[i, k, u]
        pltpu.make_async_copy(ref, ref, y_recv.at[i, k, u]).wait()
        return y_in[i, k, u].astype(F32)

    def any_of(role, roles):
        hit = role == roles[0]
        for r in roles[1:]:
            hit = hit | (role == r)
        return hit

    def pair_step(i):
        sib_copy(i).wait_recv()
        leaves = [r for r, v in tree_of(i).items() if v[0] == 1]
        for u in range(2):
            role = role_of(i, u)
            rows = slice(u * PART, (u + 1) * PART)
            value = own_part[i, rows] + sib_in[i, rows].astype(F32)
            leaf = any_of(role, leaves)

            @pl.when(leaf)
            def _():
                y_out[i, u] = value.astype(BF16)
                climb(i, u, role).start()

            @pl.when(jnp.logical_not(leaf))
            def _():
                own_part[i, rows] = value

    def tree_step(i, level):
        for u in range(2):
            role = role_of(i, u)
            rows = slice(u * PART, (u + 1) * PART)
            for count in (1, 2):
                roles = [r for r, v in tree_of(i).items() if v[0] == level and v[3] == count]
                if not roles:
                    continue

                @pl.when(any_of(role, roles))
                def _(count=count):
                    value = own_part[i, rows]
                    for k in range(count):
                        value = value + received(i, k, u)
                    y_out[i, u] = value.astype(BF16)
                    climb(i, u, role).start()

    def result(i):
        _, _, half = piece_of(i)
        cols = slice(half * COLS, (half + 1) * COLS)

        @pl.when(role_of(i, 0) == 0)
        def _():
            for u in range(2):
                rows = slice(u * PART, (u + 1) * PART)
                value = own_part[i, rows]
                for k in range(2 if i < DEEP_PIECES else 4):
                    value = value + received(i, k, u)
                value = value + b_ref[cols].astype(F32)[None, :]
                inner = 0.7978845608028654 * (value + 0.044715 * (value * value * value))
                o_ref[rows, cols] = (0.5 * value * (1.0 + jnp.tanh(inner))).astype(BF16)

    def take_tokens():
        for other in range(2):
            for s in range(4):
                mine = (other == 0) & (s == b_mine) & (c == t_core)

                @pl.when(mine)
                def _():
                    t_local().wait()

                @pl.when(jnp.logical_not(mine))
                def _(other=other, s=s):
                    ref = t_in.at[other, s]
                    pltpu.make_async_copy(ref, ref, t_recv.at[other, s]).wait()

            t_cat[other] = jnp.concatenate([t_in[other, s] for s in range(4)], axis=-1)

    for code in STEPS:
        kind, i = code // 16, code % 16
        if kind < 2:
            forward(i, kind)
        elif kind == 2:
            product(i)
        elif kind == 3:
            pair_step(i)
        elif kind < 6:
            tree_step(i, kind - 2)
        elif i == 0:
            send_tokens()
        else:
            take_tokens()

    for dz in range(1, N):
        t_copy(dz).wait_send()

    @pl.when(c != t_core)
    def _():
        t_copy(0).wait_send()

    swap_all(lambda d: d.wait_send(), None)

    for i in range(PIECES):
        hops, way, half = piece_of(i)
        for part in range(2):
            for leave in onward_ways(hops, way, half):
                w_copy(hops, leave, part, half).wait_send()
        sib_copy(i).wait_send()
        for u in range(2):
            role = role_of(i, u)

            @pl.when(role != 0)
            def _():
                climb(i, u, role).wait_send()

    for i in range(PIECES):
        result(i)


def body(tokens, up_weight, up_bias):
    return pl.pallas_call(
        kernel,
        out_shape=jax.ShapeDtypeStruct((ROWS, 512), BF16),
        in_specs=[
            pl.BlockSpec(memory_space=pltpu.HBM),
            pl.BlockSpec(memory_space=pltpu.HBM),
            pl.BlockSpec(memory_space=pltpu.VMEM),
        ],
        out_specs=pl.BlockSpec(memory_space=pltpu.VMEM),
        scratch_shapes=[
            pltpu.VMEM((2, 4, ROWS, FEAT), BF16),
            pltpu.VMEM((2, ROWS, 4 * FEAT), BF16),
            pltpu.VMEM((9, 2, 2 * HALF, COLS), BF16),
            pltpu.VMEM((PIECES, ROWS, COLS), F32),
            pltpu.VMEM((PIECES, ROWS, COLS), BF16),
            pltpu.VMEM((PIECES, ROWS, COLS), BF16),
            pltpu.VMEM((PIECES, 2, PART, COLS), BF16),
            pltpu.VMEM((PIECES, 4, 2, PART, COLS), BF16),
            pltpu.SemaphoreType.DMA((N,)),
            pltpu.SemaphoreType.DMA((2, 4)),
            pltpu.SemaphoreType.DMA((2, 2)),
            pltpu.SemaphoreType.DMA((3,)),
            pltpu.SemaphoreType.DMA((9, 2, 2)),
            pltpu.SemaphoreType.DMA((9, 2, 2)),
            pltpu.SemaphoreType.DMA((PIECES,)),
            pltpu.SemaphoreType.DMA((PIECES,)),
            pltpu.SemaphoreType.DMA((PIECES, 2)),
            pltpu.SemaphoreType.DMA((PIECES, 4, 2)),
        ],
        name="up_proj",
        compiler_params=pltpu.CompilerParams(
            collective_id=0, has_side_effects=True, vmem_limit_bytes=60 * 2**20
        ),
    )(tokens, up_weight, up_bias)


def solution(mesh):
    return jax.shard_map(
        body,
        mesh=mesh,
        in_specs=(P("depth", ("py", "px")), P("py", ("px", "depth")), P(("px", "py"))),
        out_specs=P("depth", ("px", "py")),
        check_vma=False,
    )
```
